32 devices in a mesh: groups: 1, expert: 16 (over z, y, x), hidden: 2 (over core).
Axes of the slice: x: 2, y: 2, z: 4, core: 2. Of those that a mesh axis runs over, the one named last changes fastest.
Arguments:
- tokens: bfloat16 [2048, 2048], P(('groups', 'expert')), may hold values from -6 to 6
- expert_ids: int32 [2048, 8], P(('groups', 'expert')), may hold values from 0 to 15, all different within a row; in each aligned block of 128 rows (0 to 127, 128 to 255, ...) at most 80 rows name the same one
- route_weights: float32 [2048, 8], P(('groups', 'expert')), may hold values from 0.05 to 1
- cotangent: bfloat16 [2048, 2048], P(('groups', 'expert')), may hold values from -6 to 6
- w_gate_up: bfloat16 [16, 2, 2048, 768], P('expert', None, None, 'hidden'), may hold values from -0.125 to 0.125
- w_down: bfloat16 [16, 768, 2048], P('expert', 'hidden'), may hold values from -0.21875 to 0.21875
Outputs:
- mixed: bfloat16 [2048, 2048], P(('groups', 'expert'))
- grad_tokens: bfloat16 [2048, 2048], P(('groups', 'expert'))
- grad_route: float32 [2048, 8], P(('groups', 'expert'))
- grad_down: bfloat16 [16, 768, 2048], P(('groups', 'expert'), 'hidden')
The draws below stay inside these ranges and needn't reach their ends.
Inputs may be any that keep to these rules, and one draw needn't show every extreme that they name: `expert_ids`: each token names 8 different experts; the 128 rows of one index of expert name any one expert at most 80 times.
All inputs are finite; a program needn't handle non-finite values.
Results may differ from the reference program's by a relative error of at most 0.013.
Values may be sent and summed in bfloat16 or wider, within the bound.
A program may use at most 128 MiB of HBM per device.

```python
import math
import jax
import jax.numpy as jnp
import numpy as np
from jax import lax

D = 2048
FF = 768
TOPK = 8
TOK_DEV = 128
EXPERTS = 16
CAP = 80
TOKENS = 2048
N_EXPERT = 16
N_HIDDEN = 2


def block_levels(key, shape, pieces, smallest, largest):
    def one(position, shards_of):
        draws = jax.random.uniform(jax.random.fold_in(jax.random.fold_in(key, 6), position), (shards_of,), jnp.float32, smallest / len(pieces), largest / len(pieces))
        return jnp.repeat(jnp.exp(draws), shape[position] // shards_of).reshape((-1,) + (1,) * (len(shape) - position - 1))

    level = one(*pieces[0])
    for cut in pieces[1:]:
        level = level * one(*cut)
    return level


def deal_out(stream_key, own, number, rows, count, top, limit, skew):
    order = jax.random.permutation(stream_key, count)
    heavy_load, ordinary = portions_of(count, rows * top, limit, skew, True), portions_of(count, rows * top, limit, skew, False)
    places = jnp.arange(count)

    def named(lengths, offset_by):
        used = int((lengths > 0).sum())
        fixed = max(1, used // 4)
        passed = fixed + (places - fixed + offset_by * (used - fixed)) % max(1, count - fixed)
        return jnp.zeros((count,), jnp.int32).at[order[jnp.where(places < fixed, places, passed)]].set(jnp.asarray(lengths, jnp.int32))

    lengths = jnp.where(number % 4 == 0, named(heavy_load, number // 4), named(ordinary, number - number // 4 - 1))
    mixed = jax.random.permutation(jax.random.fold_in(own, 3), count)
    giver, receiver = mixed[0:count // 2 * 2:2], mixed[1:count // 2 * 2:2]
    margin = jnp.minimum(lengths[giver] - 1, limit - lengths[receiver]) // 2
    margin = jnp.where((giver == order[0]) | (receiver == order[0]) | (lengths[receiver] == 0), 0, jnp.maximum(margin, 0))
    passed = jax.random.randint(jax.random.fold_in(own, 4), (count // 2,), 0, 1 << 20) % (margin + 1)
    lengths = lengths.at[giver].add(-passed).at[receiver].add(passed)
    labels = jnp.searchsorted(jnp.cumsum(lengths), jnp.arange(rows * top), side="right").astype(jnp.int32)
    grid = labels.reshape(top, rows).T
    grid = grid[jax.random.permutation(jax.random.fold_in(own, 1), rows)]
    offset_by = jax.random.randint(jax.random.fold_in(own, 2), (rows, 1), 0, top)
    return jnp.take_along_axis(grid, (jnp.arange(top)[None, :] + offset_by) % top, axis=1)


def portions_of(amount, total, most, lean, full):
    portions = [(1 << 20) // math.isqrt(rank ** lean) + 1 for rank in range(1, amount + 1)]
    largest = most if full else min(most, max(-(-total // amount), total * portions[0] // sum(portions)))
    least = 1 if total - largest >= amount - 1 else 0
    given, surplus = [largest] + [least] * (amount - 1), total - largest - least * (amount - 1)
    while surplus > 0:
        movable = [i for i in range(1, amount) if given[i] < largest] or [i for i in range(1, amount) if given[i] < most]
        whole, left = sum([portions[i] for i in movable]), surplus
        for i in movable:
            extra = min(most - given[i], max(1, left * portions[i] // whole), surplus)
            given[i] = given[i] + extra
            surplus = surplus - extra
    return np.array(given)


def bell_draw(key, extent, deviation, limit, split=(), held_as=jnp.bfloat16):
    entries = jax.random.normal(key, extent, jnp.float32) * deviation
    if len(split) > 0:
        entries = block_levels(key, extent, split, -0.22, 0.18) * entries
    return jnp.clip(entries, min=-limit, max=limit).astype(held_as)


def setup_inputs(seed: int = 0, part: int = 0) -> dict:
    keys = jax.random.split(jax.random.key(seed), 7)
    part_splits = jax.random.split(jax.random.fold_in(keys[6], part), 7)
    tokens = bell_draw(part_splits[0], (TOKENS, D), 1.0, 6.0, ((0, 16),))
    expert_ids_keys = jax.random.split(jax.random.fold_in(part_splits[1], 1), TOKENS // TOK_DEV)
    expert_ids_turns = jax.random.permutation(jax.random.fold_in(part_splits[1], 3), TOKENS // TOK_DEV)
    expert_ids = jax.vmap(lambda own, number: deal_out(jax.random.fold_in(part_splits[1], 2), own, number, TOK_DEV, EXPERTS, TOPK, CAP, 2))(expert_ids_keys, expert_ids_turns).reshape((TOKENS, TOPK))
    route_weights = jnp.clip(jnp.exp(math.log(1.0) - 2.9957323 * jax.random.uniform(part_splits[2], (TOKENS, TOPK), jnp.float32) ** block_levels(part_splits[2], (TOKENS, TOPK), ((0, 16),), -0.2, 0.2)), 0.05, 1.0)
    cotangent = bell_draw(part_splits[3], (TOKENS, D), 1.0, 6.0, ((0, 16),))
    w_gate_up = bell_draw(keys[4], (EXPERTS, 2, D, FF), D ** -0.5, 0.125, ((0, 16), (3, 2)))
    w_down = bell_draw(keys[5], (EXPERTS, FF, D), FF ** -0.5, 0.21875, ((0, 16), (1, 2)))
    return dict(tokens=tokens, expert_ids=expert_ids, route_weights=route_weights, cotangent=cotangent, w_gate_up=w_gate_up, w_down=w_down)


def reference(tokens, expert_ids, route_weights, cotangent, w_gate_up, w_down):
    assigned = TOKENS * TOPK
    capacity = N_EXPERT * CAP
    per_half = FF // N_HIDDEN
    flat_ids = expert_ids.reshape(assigned).astype(jnp.int32)
    order = jnp.argsort(flat_ids, stable=True).astype(jnp.int32)
    order_pad = jnp.concatenate([order, jnp.full((capacity,), assigned, jnp.int32)])
    counts = jnp.sum((flat_ids[:, None] == jnp.arange(EXPERTS, dtype=jnp.int32)[None, :]).astype(jnp.int32), 0)
    starts = (jnp.cumsum(counts) - counts).astype(jnp.int32)
    route_flat = route_weights.reshape(assigned)

    def one_expert(expert):
        picked = lax.dynamic_slice_in_dim(order_pad, starts[expert], capacity)
        valid = jnp.arange(capacity, dtype=jnp.int32) < counts[expert]
        picked = jnp.where(valid, picked, assigned).astype(jnp.int32)
        token_of = jnp.minimum(picked // TOPK, TOKENS - 1)
        rows = jnp.where(valid[:, None], tokens[token_of], jnp.zeros((), tokens.dtype))
        weight_of = jnp.where(valid, route_flat[jnp.minimum(picked, assigned - 1)], jnp.zeros((), route_flat.dtype))
        scaled = (weight_of[:, None] * cotangent[token_of].astype(jnp.float32)).astype(jnp.bfloat16)
        gate_w = w_gate_up[expert, 0]
        up_w = w_gate_up[expert, 1]
        down_mat = w_down[expert]
        gate_val = jnp.dot(rows, gate_w, preferred_element_type=jnp.float32)
        up_val = jnp.dot(rows, up_w, preferred_element_type=jnp.float32)
        sigma = jax.nn.sigmoid(gate_val)
        hidden_act = (gate_val * sigma * up_val).astype(jnp.bfloat16)
        grad_hidden = jnp.dot(scaled, down_mat.T, preferred_element_type=jnp.float32)
        grad_gate = (grad_hidden * up_val * sigma * (1.0 + gate_val * (1.0 - sigma))).astype(jnp.bfloat16)
        grad_up = (grad_hidden * gate_val * sigma).astype(jnp.bfloat16)
        out_sum = jnp.zeros((capacity, D), jnp.float32)
        grad_sum = jnp.zeros((capacity, D), jnp.float32)
        for half in range(N_HIDDEN):
            lower = half * per_half
            upper = lower + per_half
            part = jnp.dot(hidden_act[:, lower:upper], down_mat[lower:upper], preferred_element_type=jnp.float32).astype(jnp.bfloat16)
            out_sum = out_sum + lax.optimization_barrier(part).astype(jnp.float32)
            grad_part = jnp.dot(grad_gate[:, lower:upper], gate_w[:, lower:upper].T, preferred_element_type=jnp.float32)
            grad_part = grad_part + jnp.dot(grad_up[:, lower:upper], up_w[:, lower:upper].T, preferred_element_type=jnp.float32)
            grad_sum = grad_sum + lax.optimization_barrier(grad_part.astype(jnp.bfloat16)).astype(jnp.float32)
        down_grad = jnp.dot(hidden_act.T, scaled, preferred_element_type=jnp.float32).astype(jnp.bfloat16)
        return picked, out_sum.astype(jnp.bfloat16), grad_sum.astype(jnp.bfloat16), down_grad

    picked, out_rows, grad_rows, grad_down = lax.map(one_expert, jnp.arange(EXPERTS, dtype=jnp.int32))
    flat_picked = picked.reshape(EXPERTS * capacity)
    out_all = jnp.zeros((assigned + 1, D), jnp.bfloat16).at[flat_picked].set(out_rows.reshape(EXPERTS * capacity, D))[:assigned]
    grad_all = jnp.zeros((assigned + 1, D), jnp.bfloat16).at[flat_picked].set(grad_rows.reshape(EXPERTS * capacity, D))[:assigned]
    out_each = out_all.reshape(TOKENS, TOPK, D).astype(jnp.float32)
    grad_each = grad_all.reshape(TOKENS, TOPK, D).astype(jnp.float32)
    mixed = jnp.sum(out_each * route_weights[:, :, None], 1).astype(jnp.bfloat16)
    grad_route = jnp.sum(out_each * cotangent.astype(jnp.float32)[:, None, :], 2)
    grad_tokens = jnp.sum(grad_each, 1).astype(jnp.bfloat16)
    return (mixed, grad_tokens, grad_route, grad_down)
```

```python
import functools

import jax
import jax.numpy as jnp
from jax import lax
from jax.experimental import pallas as pl
from jax.experimental.pallas import tpu as pltpu
from jax.sharding import PartitionSpec as P

MESH = pl.DeviceIdType.MESH
PLANE = 4
F32 = jnp.float32
BF16 = jnp.bfloat16


def flip(a, k, size):
    out, bit = 0, 1
    while bit < size:
        digit = (a // bit) % 2
        out = out + bit * ((1 - digit) if (k // bit) % 2 else digit)
        bit *= 2
    return out


def place(planes):
    g, e, h = lax.axis_index("groups"), lax.axis_index("expert"), lax.axis_index("hidden")
    return g, e, h, e // PLANE, e % PLANE


def greet(n, g, e, h):
    barrier = pltpu.get_barrier_semaphore()

    def hello(i, _):
        to = (e + i) % n
        pl.semaphore_signal(barrier, inc=1, device_id=(g, to, h), device_id_type=MESH)
        pl.semaphore_signal(barrier, inc=1, device_id=(g, to, 1 - h), device_id_type=MESH)
        return 0

    lax.fori_loop(1, n, hello, 0)
    pl.semaphore_signal(barrier, inc=1, device_id=(g, e, 1 - h), device_id_type=MESH)
    pl.semaphore_wait(barrier, 2 * n - 1)


def gather_kernel(n, tok, cot, meta_in, gt, gc, meta, zs, zr, ps, pr, hs, hr, ms, mr, ls):
    planes = n // PLANE
    g, e, h, a, b = place(planes)
    near = [flip(b, 1, PLANE), flip(b, 2, PLANE)]
    ins, outs = (tok, cot), (gt, gc)
    greet(n, g, e, h)

    def rcopy(src, dst, s, r, to):
        return pltpu.make_async_remote_copy(
            src_ref=src, dst_ref=dst, send_sem=s, recv_sem=r, device_id=to, device_id_type=MESH
        )

    pending = []

    def go(copy):
        copy.start()
        pending.append(copy)
        return copy

    z = {}
    for k in range(1, planes):
        ak = flip(a, k, planes)
        for c in range(2):
            z[c, k] = go(rcopy(ins[c].at[h], outs[c].at[a, b, h], zs.at[c, k], zr.at[c, k],
                               (g, ak * PLANE + b, h)))

    def meta_copy(i):
        to = (e + i) % n
        return rcopy(meta_in.at[to], meta.at[e], ms.at[i], mr.at[i], (g, to, h))

    def send_meta(i, _):
        meta_copy(i).start()
        return 0

    def wait_meta(i, _):
        meta_copy(i).wait()
        return 0

    lax.fori_loop(1, n, send_meta, 0)
    local = [
        pltpu.make_async_copy(tok, gt.at[a, b], ls.at[0]),
        pltpu.make_async_copy(cot, gc.at[a, b], ls.at[1]),
        pltpu.make_async_copy(meta_in.at[e], meta.at[e], ls.at[2]),
    ]
    for copy in local:
        copy.start()

    hops, sib = {}, {}

    def hop(c, k, j, src, dst, to):
        hops[c, k, j] = go(rcopy(src, dst, ps.at[c, k, j], pr.at[c, k, j], to))

    def across(c, k, q, bq):
        ak = flip(a, k, planes)
        block = outs[c].at[ak, bq, h]
        sib[c, k, q] = go(rcopy(block, block, hs.at[c, k, q], hr.at[c, k, q], (g, e, 1 - h)))

    for k in range(planes + 2):
        if k < planes:
            ak = flip(a, k, planes)
            for c in range(2):
                first, second = near[c], near[1 - c]
                if k:
                    z[c, k].wait_recv()
                src = outs[c].at[ak, b, h] if k else ins[c].at[h]
                dst = outs[c].at[ak, b, h]
                hop(c, k, 0, src, dst, (g, a * PLANE + first, h))
                hop(c, k, 1, src, dst, (g, a * PLANE + second, h))
                if k:
                    across(c, k, 0, b)
        if 1 <= k <= planes:
            kk = k - 1
            ak = flip(a, kk, planes)
            for c in range(2):
                first, second = near[c], near[1 - c]
                hops[c, kk, 0].wait_recv()
                block = outs[c].at[ak, first, h]
                hop(c, kk, 2, block, block, (g, a * PLANE + second, h))
                across(c, kk, 1, first)
        if k >= 2:
            kk = k - 2
            for c in range(2):
                hops[c, kk, 1].wait_recv()
                across(c, kk, 2, near[1 - c])
                hops[c, kk, 2].wait_recv()
                across(c, kk, 3, flip(b, 3, PLANE))
    for copy in sib.values():
        copy.wait_recv()
    for copy in pending:
        copy.wait_send()
    lax.fori_loop(1, n, wait_meta, 0)
    for copy in local:
        copy.wait()


def gather(n, tok, cot, meta_in):
    planes = n // PLANE
    rows, width = tok.shape
    halves = (2, rows // 2, width)
    dma = pltpu.SemaphoreType.DMA
    anyspace = pl.BlockSpec(memory_space=pl.ANY)
    out = jax.ShapeDtypeStruct((planes, PLANE) + halves, BF16)
    return pl.pallas_call(
        functools.partial(gather_kernel, n),
        out_shape=(out, out, jax.ShapeDtypeStruct(meta_in.shape, F32)),
        in_specs=[anyspace] * 3,
        out_specs=(anyspace,) * 3,
        scratch_shapes=[
            dma((2, planes)), dma((2, planes)),
            dma((2, planes, 3)), dma((2, planes, 3)),
            dma((2, planes, 4)), dma((2, planes, 4)),
            dma((n,)), dma((n,)), dma((3,)),
        ],
        compiler_params=pltpu.CompilerParams(collective_id=0, has_side_effects=True),
        name="gather_rows",
    )(tok.reshape(halves), cot.reshape(halves), meta_in)


def reduce_kernel(n, pm, pg, route_in, om, og, route_out,
                  own, hbuf, nbuf, sbuf, zbuf, res,
                  os_, hs, hr, xs, xr, ys, yr, zs, zr, fs, fr, ms, mr, ls):
    planes = n // PLANE
    g, e, h, a, b = place(planes)
    near = [flip(b, 1, PLANE), flip(b, 2, PLANE)]
    opposite = flip(b, 3, PLANE)
    ins, outs = (pm, pg), (om, og)
    greet(n, g, e, h)

    def rcopy(src, dst, s, r, to):
        return pltpu.make_async_remote_copy(
            src_ref=src, dst_ref=dst, send_sem=s, recv_sem=r, device_id=to, device_id_type=MESH
        )

    pending = []

    def go(copy):
        copy.start()
        pending.append(copy)
        return copy

    def total(*parts):
        acc = parts[0].astype(F32)
        for part in parts[1:]:
            acc = acc + part.astype(F32)
        return acc.astype(BF16)

    order = list(range(1, planes)) + [0]
    load, sib = {}, {}
    for k in order:
        ak = flip(a, k, planes)
        for c in range(2):
            sib[c, k] = go(rcopy(ins[c].at[ak, :, 1 - h], hbuf.at[c, k], hs.at[c, k], hr.at[c, k],
                                 (g, e, 1 - h)))
            load[c, k] = pltpu.make_async_copy(ins[c].at[ak, :, h], own.at[c, k], os_.at[c, k])
            load[c, k].start()

    def route_copy(i, j):
        to = (e + i) % n
        return rcopy(route_in.at[to], route_out.at[e, h], ms.at[i, j], mr.at[i, j],
                     (g, to, (h + j) % 2))

    def send_route(i, _):
        route_copy(i, 0).start()
        route_copy(i, 1).start()
        return 0

    def wait_route(i, _):
        route_copy(i, 0).wait()
        route_copy(i, 1).wait()
        return 0

    route_copy(0, 1).start()
    lax.fori_loop(1, n, send_route, 0)
    mine = pltpu.make_async_copy(route_in.at[e], route_out.at[e, h], ls.at[0])
    mine.start()

    hop1, hop2, up = {}, {}, {}
    for step in range(planes + 2):
        if step < planes:
            k = order[step]
            for c in range(2):
                first, second = near[c], near[1 - c]
                load[c, k].wait()
                sib[c, k].wait_recv()
                for j, q in enumerate((opposite, first)):
                    own[c, k, q] = total(own[c, k, q], hbuf[c, k, q])
                    hop1[c, k, j] = go(rcopy(own.at[c, k, q], nbuf.at[c, k, j], xs.at[c, k, j],
                                             xr.at[c, k, j], (g, a * PLANE + first, h)))
                for q in (second, b):
                    own[c, k, q] = total(own[c, k, q], hbuf[c, k, q])
        if 1 <= step <= planes:
            k = order[step - 1]
            for c in range(2):
                second = near[1 - c]
                hop1[c, k, 0].wait_recv()
                own[c, k, second] = total(own[c, k, second], nbuf[c, k, 0])
                hop2[c, k] = go(rcopy(own.at[c, k, second], sbuf.at[c, k], ys.at[c, k],
                                      yr.at[c, k], (g, a * PLANE + second, h)))
                hop1[c, k, 1].wait_recv()
        if step >= 2:
            k = order[step - 2]
            for c in range(2):
                hop2[c, k].wait_recv()
                if k:
                    own[c, k, b] = total(own[c, k, b], nbuf[c, k, 1], sbuf[c, k])
                    ak = flip(a, k, planes)
                    up[c, k] = go(rcopy(own.at[c, k, b], zbuf.at[c, k], zs.at[c, k], zr.at[c, k],
                                        (g, ak * PLANE + b, h)))
    final = {}
    store = []
    for c in range(2):
        for k in range(1, planes):
            up[c, k].wait_recv()
        res[c] = total(own[c, 0, b], nbuf[c, 0, 1], sbuf[c, 0],
                       *[zbuf[c, k] for k in range(1, planes)])
        final[c] = go(rcopy(res.at[c], outs[c].at[h], fs.at[c], fr.at[c], (g, e, 1 - h)))
        copy = pltpu.make_async_copy(res.at[c], outs[c].at[h], ls.at[1 + c])
        copy.start()
        store.append(copy)
    for c in range(2):
        final[c].wait_recv()
        store[c].wait()
    for copy in pending:
        copy.wait_send()
    mine.wait()
    route_copy(0, 1).wait()
    lax.fori_loop(1, n, wait_route, 0)


def reduce_rows(n, part, mixed, grad, route, call_id):
    planes = n // PLANE
    width = mixed.shape[1]
    half = part // 2
    dma = pltpu.SemaphoreType.DMA
    anyspace = pl.BlockSpec(memory_space=pl.ANY)
    view = (planes, PLANE, 2, half, width)
    out = jax.ShapeDtypeStruct((2, half, width), BF16)
    vm = lambda *lead: pltpu.VMEM(lead + (half, width), BF16)
    om, og, ro = pl.pallas_call(
        functools.partial(reduce_kernel, n),
        out_shape=(out, out, jax.ShapeDtypeStruct((n, 2) + route.shape[1:], F32)),
        in_specs=[anyspace] * 3,
        out_specs=(anyspace,) * 3,
        scratch_shapes=[
            vm(2, planes, PLANE), vm(2, planes, PLANE), vm(2, planes, 2), vm(2, planes),
            vm(2, planes), vm(2),
            dma((2, planes)),
            dma((2, planes)), dma((2, planes)),
            dma((2, planes, 2)), dma((2, planes, 2)),
            dma((2, planes)), dma((2, planes)),
            dma((2, planes)), dma((2, planes)),
            dma((2,)), dma((2,)),
            dma((n, 2)), dma((n, 2)), dma((3,)),
        ],
        compiler_params=pltpu.CompilerParams(
            collective_id=call_id, has_side_effects=True, vmem_limit_bytes=48 * 2**20
        ),
        name="reduce_rows",
    )(mixed.reshape(view), grad.reshape(view), route)
    return om.reshape(part, width), og.reshape(part, width), ro


def shards(tokens, expert_ids, route_weights, cotangent, w_gate_up, w_down):
    part, features = tokens.shape
    n = lax.axis_size("expert")
    chosen = (expert_ids[:, :, None] == jnp.arange(n, dtype=jnp.int32)).astype(F32)
    dense = jnp.sum(chosen * route_weights[:, :, None], 1)
    meta_in = jnp.broadcast_to(dense.T[:, None, :], (n, 8, part))
    gt, gc, meta = gather(n, tokens, cotangent, meta_in)
    x_rows = gt.reshape(n * part, features)
    d_rows = gc.reshape(n * part, features)
    weight = meta[:, 0, :].reshape(n * part, 1)
    gate_w, up_w, down = w_gate_up[0, 0], w_gate_up[0, 1], w_down[0]
    gate = jnp.dot(x_rows, gate_w, preferred_element_type=F32)
    up = jnp.dot(x_rows, up_w, preferred_element_type=F32)
    grad_act = jnp.einsum("rd,fd->rf", d_rows, down, preferred_element_type=F32)
    sig = jax.nn.sigmoid(gate)
    act = gate * sig * up
    route = jnp.sum(act * grad_act, 1).reshape(n, 1, part)
    act_w = (act * weight).astype(BF16)
    grad_w = grad_act * weight
    grad_gate = (grad_w * up * sig * (1.0 + gate * (1.0 - sig))).astype(BF16)
    grad_up = (grad_w * gate * sig).astype(BF16)
    grad_down = jnp.einsum("rf,rd->fd", act_w, d_rows, preferred_element_type=F32).astype(BF16)
    route_in = jnp.broadcast_to(route, (n, 8, part))
    cuts = max(1, n // 16)
    step = features // cuts
    mixed, grad = [], []
    for i in range(cuts):
        cols = slice(i * step, (i + 1) * step)
        mixed_part = jnp.dot(act_w, down[:, cols], preferred_element_type=F32).astype(BF16)
        grad_part = (
            jnp.einsum("rf,df->rd", grad_gate, gate_w[cols], preferred_element_type=F32)
            + jnp.einsum("rf,df->rd", grad_up, up_w[cols], preferred_element_type=F32)
        ).astype(BF16)
        m, gr, ro = reduce_rows(n, part, mixed_part, grad_part, route_in, 1 + i)
        mixed.append(m)
        grad.append(gr)
        if i == 0:
            by_expert = ro[:, 0, 0] + ro[:, 1, 0]
        if i + 1 < cuts:
            m, gr, act_w, grad_gate, grad_up = lax.optimization_barrier(
                (m, gr, act_w, grad_gate, grad_up)
            )
    grad_route = jnp.sum(chosen * by_expert.T[:, None, :], 2)
    if cuts > 1:
        return (jnp.concatenate(mixed, 1), jnp.concatenate(grad, 1), grad_route, grad_down[None])
    return (mixed[0], grad[0], grad_route, grad_down[None])


def solution(mesh):
    rows = P(("groups", "expert"), None)
    return jax.shard_map(
        shards,
        mesh=mesh,
        in_specs=(rows, rows, rows, rows, P("expert", None, None, "hidden"), P("expert", "hidden", None)),
        out_specs=(rows, rows, rows, P(("groups", "expert"), "hidden", None)),
        check_vma=False,
    )
```

```python
import functools

import jax
import jax.numpy as jnp
from jax import lax
from jax.experimental import pallas as pl
from jax.experimental.pallas import tpu as pltpu
from jax.sharding import PartitionSpec as P

MESH = pl.DeviceIdType.MESH
PLANE = 4
F32 = jnp.float32
BF16 = jnp.bfloat16


def flip(a, k, size):
    out, bit = 0, 1
    while bit < size:
        digit = (a // bit) % 2
        out = out + bit * ((1 - digit) if (k // bit) % 2 else digit)
        bit *= 2
    return out


def place(planes):
    g, e, h = lax.axis_index("groups"), lax.axis_index("expert"), lax.axis_index("hidden")
    return g, e, h, e // PLANE, e % PLANE


def greet(n, g, e, h):
    barrier = pltpu.get_barrier_semaphore()

    def hello(i, _):
        to = (e + i) % n
        pl.semaphore_signal(barrier, inc=1, device_id=(g, to, h), device_id_type=MESH)
        pl.semaphore_signal(barrier, inc=1, device_id=(g, to, 1 - h), device_id_type=MESH)
        return 0

    lax.fori_loop(1, n, hello, 0)
    pl.semaphore_signal(barrier, inc=1, device_id=(g, e, 1 - h), device_id_type=MESH)
    pl.semaphore_wait(barrier, 2 * n - 1)


def gather_kernel(n, tok, cot, meta_in, gt, gc, meta, zs, zr, ps, pr, hs, hr, ms, mr, ls):
    planes = n // PLANE
    g, e, h, a, b = place(planes)
    near = [flip(b, 1, PLANE), flip(b, 2, PLANE)]
    ins, outs = (tok, cot), (gt, gc)
    greet(n, g, e, h)

    def rcopy(src, dst, s, r, to):
        return pltpu.make_async_remote_copy(
            src_ref=src, dst_ref=dst, send_sem=s, recv_sem=r, device_id=to, device_id_type=MESH
        )

    pending = []

    def go(copy):
        copy.start()
        pending.append(copy)
        return copy

    z = {}
    for k in range(1, planes):
        ak = flip(a, k, planes)
        for c in range(2):
            z[c, k] = go(rcopy(ins[c].at[h], outs[c].at[a, b, h], zs.at[c, k], zr.at[c, k],
                               (g, ak * PLANE + b, h)))

    def meta_copy(i):
        to = (e + i) % n
        return rcopy(meta_in.at[to], meta.at[e], ms.at[i], mr.at[i], (g, to, h))

    def send_meta(i, _):
        meta_copy(i).start()
        return 0

    def wait_meta(i, _):
        meta_copy(i).wait()
        return 0

    lax.fori_loop(1, n, send_meta, 0)
    local = [
        pltpu.make_async_copy(tok, gt.at[a, b], ls.at[0]),
        pltpu.make_async_copy(cot, gc.at[a, b], ls.at[1]),
        pltpu.make_async_copy(meta_in.at[e], meta.at[e], ls.at[2]),
    ]
    for copy in local:
        copy.start()

    hops, sib = {}, {}

    def hop(c, k, j, src, dst, to):
        hops[c, k, j] = go(rcopy(src, dst, ps.at[c, k, j], pr.at[c, k, j], to))

    def across(c, k, q, bq):
        ak = flip(a, k, planes)
        block = outs[c].at[ak, bq, h]
        sib[c, k, q] = go(rcopy(block, block, hs.at[c, k, q], hr.at[c, k, q], (g, e, 1 - h)))

    for k in range(planes + 2):
        if k < planes:
            ak = flip(a, k, planes)
            for c in range(2):
                first, second = near[c], near[1 - c]
                if k:
                    z[c, k].wait_recv()
                src = outs[c].at[ak, b, h] if k else ins[c].at[h]
                dst = outs[c].at[ak, b, h]
                hop(c, k, 0, src, dst, (g, a * PLANE + first, h))
                hop(c, k, 1, src, dst, (g, a * PLANE + second, h))
                if k:
                    across(c, k, 0, b)
        if 1 <= k <= planes:
            kk = k - 1
            ak = flip(a, kk, planes)
            for c in range(2):
                first, second = near[c], near[1 - c]
                hops[c, kk, 0].wait_recv()
                block = outs[c].at[ak, first, h]
                hop(c, kk, 2, block, block, (g, a * PLANE + second, h))
                across(c, kk, 1, first)
        if k >= 2:
            kk = k - 2
            for c in range(2):
                hops[c, kk, 1].wait_recv()
                across(c, kk, 2, near[1 - c])
                hops[c, kk, 2].wait_recv()
                across(c, kk, 3, flip(b, 3, PLANE))
    for copy in sib.values():
        copy.wait_recv()
    for copy in pending:
        copy.wait_send()
    lax.fori_loop(1, n, wait_meta, 0)
    for copy in local:
        copy.wait()


def gather(n, tok, cot, meta_in):
    planes = n // PLANE
    rows, width = tok.shape
    halves = (2, rows // 2, width)
    dma = pltpu.SemaphoreType.DMA
    anyspace = pl.BlockSpec(memory_space=pl.ANY)
    out = jax.ShapeDtypeStruct((planes, PLANE) + halves, BF16)
    return pl.pallas_call(
        functools.partial(gather_kernel, n),
        out_shape=(out, out, jax.ShapeDtypeStruct(meta_in.shape, F32)),
        in_specs=[anyspace] * 3,
        out_specs=(anyspace,) * 3,
        scratch_shapes=[
            dma((2, planes)), dma((2, planes)),
            dma((2, planes, 3)), dma((2, planes, 3)),
            dma((2, planes, 4)), dma((2, planes, 4)),
            dma((n,)), dma((n,)), dma((3,)),
        ],
        compiler_params=pltpu.CompilerParams(collective_id=0, has_side_effects=True),
        name="gather_rows",
    )(tok.reshape(halves), cot.reshape(halves), meta_in)


def reduce_kernel(n, act_ref, gg_ref, gu_ref, down_ref, gw_ref, uw_ref, route_in, om, og, route_out,
                  own, pbuf, hbuf, nbuf, sbuf, zbuf, res,
                  hs, hr, xs, xr, ys, yr, zs, zr, fs, fr, ms, mr, ls):
    planes = n // PLANE
    g, e, h, a, b = place(planes)
    near = [flip(b, 1, PLANE), flip(b, 2, PLANE)]
    opposite = flip(b, 3, PLANE)
    outs = (om, og)
    greet(n, g, e, h)

    def rcopy(src, dst, s, r, to):
        return pltpu.make_async_remote_copy(
            src_ref=src, dst_ref=dst, send_sem=s, recv_sem=r, device_id=to, device_id_type=MESH
        )

    pending = []

    def go(copy):
        copy.start()
        pending.append(copy)
        return copy

    def total(*parts):
        acc = parts[0].astype(F32)
        for part in parts[1:]:
            acc = acc + part.astype(F32)
        return acc.astype(BF16)

    order = list(range(1, planes)) + [0]
    sib = {}
    half = own.shape[3]
    group = PLANE * 2 * half
    tile = 256

    def partial(k):
        rows = pl.ds(pl.multiple_of(flip(a, k, planes) * group, group), group)
        act, gg, gu = act_ref[rows, :], gg_ref[rows, :], gu_ref[rows, :]

        def columns(t, _):
            cols = pl.ds(pl.multiple_of(t * tile, tile), tile)
            nt = (((1,), (1,)), ((), ()))
            mixed = jnp.dot(act, down_ref[:, cols], preferred_element_type=F32)
            grad = lax.dot_general(gg, gw_ref[cols, :], nt, preferred_element_type=F32)
            grad = grad + lax.dot_general(gu, uw_ref[cols, :], nt, preferred_element_type=F32)
            for c, term in enumerate((mixed, grad)):
                term = term.astype(BF16).reshape(PLANE, 2, half, tile)
                low, high = term[:, 0], term[:, 1]
                own[c, k, :, :, cols] = jnp.where(h == 0, low, high)
                pbuf[c, k, :, :, cols] = jnp.where(h == 0, high, low)
            return 0

        lax.fori_loop(0, own.shape[4] // tile, columns, 0)
        for c in range(2):
            sib[c, k] = go(rcopy(pbuf.at[c, k], hbuf.at[c, k], hs.at[c, k], hr.at[c, k],
                                 (g, e, 1 - h)))

    def route_copy(i, j):
        to = (e + i) % n
        return rcopy(route_in.at[to], route_out.at[e, h], ms.at[i, j], mr.at[i, j],
                     (g, to, (h + j) % 2))

    def send_route(i, _):
        route_copy(i, 0).start()
        route_copy(i, 1).start()
        return 0

    def wait_route(i, _):
        route_copy(i, 0).wait()
        route_copy(i, 1).wait()
        return 0

    route_copy(0, 1).start()
    lax.fori_loop(1, n, send_route, 0)
    mine = pltpu.make_async_copy(route_in.at[e], route_out.at[e, h], ls.at[0])
    mine.start()

    hop1, hop2, up = {}, {}, {}
    partial(order[0])
    for step in range(planes + 2):
        if step + 1 < planes:
            partial(order[step + 1])
        if step < planes:
            k = order[step]
            for c in range(2):
                first, second = near[c], near[1 - c]
                sib[c, k].wait_recv()
                for j, q in enumerate((opposite, first)):
                    own[c, k, q] = total(own[c, k, q], hbuf[c, k, q])
                    hop1[c, k, j] = go(rcopy(own.at[c, k, q], nbuf.at[c, k, j], xs.at[c, k, j],
                                             xr.at[c, k, j], (g, a * PLANE + first, h)))
                for q in (second, b):
                    own[c, k, q] = total(own[c, k, q], hbuf[c, k, q])
        if 1 <= step <= planes:
            k = order[step - 1]
            for c in range(2):
                second = near[1 - c]
                hop1[c, k, 0].wait_recv()
                own[c, k, second] = total(own[c, k, second], nbuf[c, k, 0])
                hop2[c, k] = go(rcopy(own.at[c, k, second], sbuf.at[c, k], ys.at[c, k],
                                      yr.at[c, k], (g, a * PLANE + second, h)))
                hop1[c, k, 1].wait_recv()
        if step >= 2:
            k = order[step - 2]
            for c in range(2):
                hop2[c, k].wait_recv()
                if k:
                    own[c, k, b] = total(own[c, k, b], nbuf[c, k, 1], sbuf[c, k])
                    ak = flip(a, k, planes)
                    up[c, k] = go(rcopy(own.at[c, k, b], zbuf.at[c, k], zs.at[c, k], zr.at[c, k],
                                        (g, ak * PLANE + b, h)))
    final = {}
    store = []
    for c in range(2):
        for k in range(1, planes):
            up[c, k].wait_recv()
        res[c] = total(own[c, 0, b], nbuf[c, 0, 1], sbuf[c, 0],
                       *[zbuf[c, k] for k in range(1, planes)])
        final[c] = go(rcopy(res.at[c], outs[c].at[h], fs.at[c], fr.at[c], (g, e, 1 - h)))
        copy = pltpu.make_async_copy(res.at[c], outs[c].at[h], ls.at[1 + c])
        copy.start()
        store.append(copy)
    for c in range(2):
        final[c].wait_recv()
        store[c].wait()
    for copy in pending:
        copy.wait_send()
    mine.wait()
    route_copy(0, 1).wait()
    lax.fori_loop(1, n, wait_route, 0)


def reduce_rows(n, part, act, gg, gu, down, gate_w, up_w, route, call_id):
    planes = n // PLANE
    width = down.shape[1]
    half = part // 2
    dma = pltpu.SemaphoreType.DMA
    anyspace = pl.BlockSpec(memory_space=pl.ANY)
    inside = pl.BlockSpec(memory_space=pltpu.VMEM)
    out = jax.ShapeDtypeStruct((2, half, width), BF16)
    vm = lambda *lead: pltpu.VMEM(lead + (half, width), BF16)
    om, og, ro = pl.pallas_call(
        functools.partial(reduce_kernel, n),
        out_shape=(out, out, jax.ShapeDtypeStruct((n, 2) + route.shape[1:], F32)),
        in_specs=[inside] * 6 + [anyspace],
        out_specs=(anyspace,) * 3,
        scratch_shapes=[
            vm(2, planes, PLANE), vm(2, planes, PLANE), vm(2, planes, PLANE), vm(2, planes, 2), vm(2, planes),
            vm(2, planes), vm(2),
            dma((2, planes)), dma((2, planes)),
            dma((2, planes, 2)), dma((2, planes, 2)),
            dma((2, planes)), dma((2, planes)),
            dma((2, planes)), dma((2, planes)),
            dma((2,)), dma((2,)),
            dma((n, 2)), dma((n, 2)), dma((3,)),
        ],
        compiler_params=pltpu.CompilerParams(
            collective_id=call_id, has_side_effects=True, vmem_limit_bytes=60 * 2**20
        ),
        name="reduce_rows",
    )(act, gg, gu, down, gate_w, up_w, route)
    return om.reshape(part, width), og.reshape(part, width), ro


def shards(tokens, expert_ids, route_weights, cotangent, w_gate_up, w_down):
    part, features = tokens.shape
    n = lax.axis_size("expert")
    chosen = (expert_ids[:, :, None] == jnp.arange(n, dtype=jnp.int32)).astype(F32)
    dense = jnp.sum(chosen * route_weights[:, :, None], 1)
    meta_in = jnp.broadcast_to(dense.T[:, None, :], (n, 8, part))
    gt, gc, meta = gather(n, tokens, cotangent, meta_in)
    x_rows = gt.reshape(n * part, features)
    d_rows = gc.reshape(n * part, features)
    weight = meta[:, 0, :].reshape(n * part, 1)
    gate_w, up_w, down = w_gate_up[0, 0], w_gate_up[0, 1], w_down[0]
    gate = jnp.dot(x_rows, gate_w, preferred_element_type=F32)
    up = jnp.dot(x_rows, up_w, preferred_element_type=F32)
    grad_act = jnp.einsum("rd,fd->rf", d_rows, down, preferred_element_type=F32)
    sig = jax.nn.sigmoid(gate)
    act = gate * sig * up
    route = jnp.sum(act * grad_act, 1).reshape(n, 1, part)
    act_w = (act * weight).astype(BF16)
    grad_w = grad_act * weight
    grad_gate = (grad_w * up * sig * (1.0 + gate * (1.0 - sig))).astype(BF16)
    grad_up = (grad_w * gate * sig).astype(BF16)
    grad_down = jnp.einsum("rf,rd->fd", act_w, d_rows, preferred_element_type=F32).astype(BF16)
    route_in = jnp.broadcast_to(route, (n, 8, part))
    cuts = max(1, n // 16)
    step = features // cuts
    mixed, grad = [], []
    for i in range(cuts):
        cols = slice(i * step, (i + 1) * step)
        m, gr, ro = reduce_rows(
            n, part, act_w, grad_gate, grad_up, down[:, cols], gate_w[cols], up_w[cols], route_in, 1 + i
        )
        mixed.append(m)
        grad.append(gr)
        if i == 0:
            by_expert = ro[:, 0, 0] + ro[:, 1, 0]
        if i + 1 < cuts:
            m, gr, act_w, grad_gate, grad_up = lax.optimization_barrier(
                (m, gr, act_w, grad_gate, grad_up)
            )
    grad_route = jnp.sum(chosen * by_expert.T[:, None, :], 2)
    if cuts > 1:
        return (jnp.concatenate(mixed, 1), jnp.concatenate(grad, 1), grad_route, grad_down[None])
    return (mixed[0], grad[0], grad_route, grad_down[None])


def solution(mesh):
    rows = P(("groups", "expert"), None)
    return jax.shard_map(
        shards,
        mesh=mesh,
        in_specs=(rows, rows, rows, rows, P("expert", None, None, "hidden"), P("expert", "hidden", None)),
        out_specs=(rows, rows, rows, P(("groups", "expert"), "hidden", None)),
        check_vma=False,
    )
```
